256 devices in a mesh: lon: 16 (over z, y_lo), lat: 16 (over y_hi, x, core).
Axes of the slice: x: 4, y: 4 (y_hi: 2, y_lo: 2; y = y_hi * 2 + y_lo), z: 8, core: 2. Of those that a mesh axis runs over, the one named last changes fastest.
Arguments:
- ensemble: float32 [128, 256, 2048], P(None, 'lat', 'lon'), may hold values from -6 to 6
- obs_value: float32 [6, 16, 2048], P(None, 'lat', 'lon'), may hold values from -6 to 6
- obs_error: float32 [6, 16, 2048], P(None, 'lat', 'lon'), may hold values from 0.05 to 0.5
- obs_row: int32 [6, 16, 2048], P(None, 'lat', 'lon'), may hold values from 0 to 15
- obs_col: int32 [6, 16, 2048], P(None, 'lat', 'lon'), may hold values from 1 to 126
- foot_weight: float32 [6, 16, 9, 2048], P(None, 'lat', None, 'lon'), may hold values from 0.1 to 1
- obs_count: int32 [6, 16, 16], P(None, 'lat', 'lon'), may hold values from 1 to 128, 1024 in all within a row
- batch_order: int32 [6], replicated, may hold values from 0 to 5, each once
Outputs:
- analysis: float32 [128, 256, 2048], P(None, 'lat', 'lon')
The draws below stay inside these ranges and needn't reach their ends.
Inputs may be any that keep to these rules, and one draw needn't show every extreme that they name: `obs_col`: every pixel footprint lies inside its tile's longitude columns. `obs_count`: for each batch and latitude row the counts of the longitude tiles add up to 128 * 16 // 2. `batch_order`: each batch appears once.
All inputs are finite; a program needn't handle non-finite values. No bound on the sum of `obs_count` on one device may be relied on, other than what follows from the above.
Results may differ from the reference program's by a relative error of at most 0.012.
Values may be sent and summed in bfloat16 or wider, within the bound.
No kernel may reach another device: no remote copies, remote signals or barrier semaphores. Data moves between devices by JAX's collectives and lax.ppermute only.
A program may use at most 64 MiB of HBM per device.

```python
import math
import jax
import jax.numpy as jnp
import numpy as np
from jax import lax

MEMB = 128
CLAT = 16
CLON = 128
OBS = 128
NB = 6
HOPS = 2
NLAT = 256
NLON = 2048
OBS_ROW = 2048
N_LON = 16
N_LAT = 16


def set_ends(entries, key, low, top_value):
    longest = entries.shape.index(max(entries.shape))
    spots = []
    for shift in (0, 1):
        where = [jax.random.randint(jax.random.fold_in(key, axis), (), 0, length) for axis, length in enumerate(entries.shape)]
        where[longest] = (where[longest] + shift) % entries.shape[longest]
        spots.append(tuple(where))
    return entries.at[spots[0]].set(low).at[spots[1]].set(top_value)


def shard_levels(key, dims, cuts, least, top_value):
    def one(position, blocks):
        draws = jax.random.uniform(jax.random.fold_in(jax.random.fold_in(key, 6), position), (blocks,), jnp.float32, least / len(cuts), top_value / len(cuts))
        return jnp.repeat(jnp.exp(draws), dims[position] // blocks).reshape((-1,) + (1,) * (len(dims) - position - 1))

    gain = one(*cuts[0])
    for cut in cuts[1:]:
        gain = gain * one(*cut)
    return gain


def length_profile(number_of, total, limit, slope):
    portions = [(1 << 20) // math.isqrt(rank ** slope) + 1 for rank in range(2, number_of + 1)]
    spare, given = total - limit - (number_of - 1), [1] * (number_of - 1)
    while spare > 0:
        candidates = [i for i in range(number_of - 1) if given[i] < limit]
        pool, left = sum([portions[i] for i in candidates]), spare
        for i in candidates:
            extra = min(limit - given[i], max(1, left * portions[i] // pool), spare)
            given[i] = given[i] + extra
            spare = spare - extra
    return np.array([limit] + given)


def ragged_sizes(rng, count, total, reach, slope):
    if count == 2:
        one = jax.random.randint(rng, (), max(1, total - reach), min(reach, total - 1) + 1)
        return jnp.stack([one, total - one])
    lengths = jnp.asarray(length_profile(count, total, reach, slope), jnp.int32)
    couples = (count - 1) // 2
    giver, taker = lengths[1:1 + 2 * couples:2], lengths[2:2 + 2 * couples:2]
    slack = jnp.minimum(giver - 1, reach - taker)
    passed = jax.random.randint(jax.random.fold_in(rng, 1), (couples,), 0, 1 << 20) % (slack + 1)
    lengths = lengths.at[1:1 + 2 * couples:2].set(giver - passed).at[2:2 + 2 * couples:2].set(taker + passed)
    return lengths[jax.random.permutation(jax.random.fold_in(rng, 2), count)]


def noise(stream_key, shape, scale, bound, split=(), kind=jnp.bfloat16):
    result = scale * jax.random.normal(stream_key, shape, jnp.float32)
    if split:
        result = result * shard_levels(stream_key, shape, split, -0.22, 0.18)
    return jnp.clip(result, -bound, bound).astype(kind)


def setup_inputs(seed: int = 0) -> dict:
    splits = jax.random.split(jax.random.key(seed), 9)
    return {
        "ensemble": noise(splits[0], (MEMB, NLAT, NLON), 1.0, 6.0, ((1, 16), (2, 16)), jnp.float32),
        "obs_value": noise(splits[1], (NB, N_LAT, OBS_ROW), 1.0, 6.0, ((1, 16), (2, 16)), jnp.float32),
        "obs_error": jnp.clip(jnp.exp(math.log(0.5) - 2.3025851 * jax.random.uniform(splits[2], (NB, N_LAT, OBS_ROW), jnp.float32) ** shard_levels(splits[2], (NB, N_LAT, OBS_ROW), ((1, 16), (2, 16)), -0.2, 0.2)), 0.05, 0.5),
        "obs_row": set_ends(jax.random.randint(splits[3], (NB, N_LAT, OBS_ROW), 0, CLAT), jax.random.fold_in(splits[3], 1), 0, CLAT - 1).astype(jnp.int32),
        "obs_col": set_ends(jax.random.randint(splits[4], (NB, N_LAT, OBS_ROW), 1, CLON - 1), jax.random.fold_in(splits[4], 1), 1, (CLON - 1) - 1).astype(jnp.int32),
        "foot_weight": jnp.clip(jnp.exp(math.log(1.0) - 2.3025851 * jax.random.uniform(splits[5], (NB, N_LAT, 9, OBS_ROW), jnp.float32) ** shard_levels(splits[5], (NB, N_LAT, 9, OBS_ROW), ((1, 16), (3, 16)), -0.2, 0.2)), 0.1, 1.0),
        "obs_count": jax.vmap(lambda own: ragged_sizes(own, N_LON, OBS * N_LON // 2, OBS, 2))(jax.random.split(splits[6], NB * N_LAT)).reshape((NB, N_LAT, N_LON)).astype(jnp.int32),
        "batch_order": jax.random.permutation(splits[7], NB).astype(jnp.int32),
    }


def footprint(rows_block, row_cell, col_cell, weight, col_base, width):
    flattened = rows_block.reshape(rows_block.shape[0], -1)
    summed = jnp.zeros((rows_block.shape[0], row_cell.shape[0]), jnp.float32)
    for offset in range(9):
        row_step = offset // 3 - 1
        col_step = offset % 3 - 1
        picks = ((row_cell + row_step + 1) * width + col_base + col_cell + col_step).astype(jnp.int32)
        summed = summed + weight[offset][None, :] * jnp.take(flattened, picks, axis=1)
    return summed / lax.optimization_barrier(jnp.sum(weight, axis=0))[None, :]

def reference(ensemble, obs_value, obs_error, obs_row, obs_col, foot_weight, obs_count, batch_order):
    radius = 1.0 * (HOPS * CLON + 2)
    cell_count = CLAT * CLON
    cell_row = (jnp.arange(cell_count) // CLON).astype(jnp.float32)
    cell_col = (jnp.arange(cell_count) % CLON).astype(jnp.float32)
    obs_tile = (jnp.arange(OBS_ROW) // OBS).astype(jnp.int32)
    offsets = (jnp.arange(2 * HOPS + 1) - HOPS).astype(jnp.int32)
    lon_base = jnp.repeat(offsets * CLON, OBS).astype(jnp.float32)
    state = ensemble
    for step_index in range(NB):
        batch = batch_order[step_index]
        values = obs_value[batch]
        obs_err = obs_error[batch]
        rows_now = obs_row[batch]
        cols_now = obs_col[batch]
        weights_now = foot_weight[batch]
        counts_now = obs_count[batch]
        padded = jnp.pad(state, ((0, 0), (1, 1), (0, 0)))

        def row_priors(lat_tile):
            rows_block = lax.dynamic_slice_in_dim(padded, lat_tile * CLAT, CLAT + 2, 1)
            return footprint(rows_block, rows_now[lat_tile], cols_now[lat_tile], weights_now[lat_tile], obs_tile * CLON, NLON)
        priors = lax.map(row_priors, jnp.arange(N_LAT).astype(jnp.int32))
        ybar = lax.optimization_barrier(jnp.mean(priors, axis=1))
        dev = priors - ybar[:, None, :]
        spread = lax.optimization_barrier(jnp.sum(dev * dev, axis=1)) / (MEMB - 1.0)
        inverse = 1.0 / (spread + obs_err)
        reducer = 1.0 / (1.0 + jnp.sqrt(obs_err * inverse))
        active = ((jnp.arange(OBS_ROW) % OBS)[None, :] < jnp.repeat(counts_now, OBS, axis=1)).astype(jnp.float32)
        innov = (active * (values - ybar) * inverse).astype(jnp.bfloat16)
        shrink = (active * reducer * inverse).astype(jnp.bfloat16)
        prior_dev = dev.astype(jnp.bfloat16)

        def update_tile(flat_tile):
            lat_tile = flat_tile // N_LON
            lon_tile = flat_tile % N_LON
            tile_state = lax.dynamic_slice(state, (jnp.int32(0), (lat_tile * CLAT).astype(jnp.int32), (lon_tile * CLON).astype(jnp.int32)), (MEMB, CLAT, CLON)).reshape(MEMB, cell_count)
            ens_mean = lax.optimization_barrier(jnp.mean(tile_state, axis=0))
            deviation = (tile_state - ens_mean[None, :]).astype(jnp.bfloat16)
            sources = (lon_tile + offsets) % N_LON
            picks = (sources[:, None] * OBS + jnp.arange(OBS)[None, :]).reshape(-1).astype(jnp.int32)
            block_dev = jnp.take(prior_dev[lat_tile], picks, axis=1)
            block_innov = jnp.take(innov[lat_tile], picks).astype(jnp.float32)
            block_shrink = jnp.take(shrink[lat_tile], picks).astype(jnp.float32)
            block_row = jnp.take(rows_now[lat_tile], picks).astype(jnp.float32)
            block_col = jnp.take(cols_now[lat_tile], picks).astype(jnp.float32)
            lon_gap = (lon_base + block_col)[None, :] - cell_col[:, None]
            lat_gap = block_row[None, :] - cell_row[:, None]
            taper = jnp.maximum(0.0, 1.0 - (lon_gap / radius) ** 2) * (1.0 - (lat_gap / (1.0 * CLAT)) ** 2)
            covar = jnp.dot(deviation.T, block_dev, preferred_element_type=jnp.float32) / (MEMB - 1.0)
            weighted = covar * taper
            mean_step = jnp.dot(weighted, block_innov, precision=lax.Precision.HIGHEST)
            packed = (weighted * block_shrink[None, :]).astype(jnp.bfloat16)
            pert_step = -jnp.dot(block_dev, packed.T, preferred_element_type=jnp.float32)
            return (tile_state + mean_step[None, :] + pert_step).reshape(MEMB, CLAT, CLON)
        tiles = lax.map(update_tile, jnp.arange(N_LAT * N_LON).astype(jnp.int32))
        state = tiles.reshape(N_LAT, N_LON, MEMB, CLAT, CLON).transpose(2, 0, 3, 1, 4).reshape(MEMB, NLAT, NLON)
    return state
```

```python
import functools

import jax
import jax.numpy as jnp
from jax import lax
from jax.experimental import pallas as pl
from jax.experimental.pallas import tpu as pltpu
from jax.sharding import PartitionSpec as P

NB = 6
HOPS = 2
MEMB = 128
CLAT = 16
CLON = 128
OBS = 128
HEAD = 16
WIDE = MEMB + HEAD
RADIUS = 1.0 * (HOPS * CLON + 2)
F32 = jnp.float32
BF16 = jnp.bfloat16
VMEM = pl.BlockSpec(memory_space=pltpu.VMEM)
SMEM = pl.BlockSpec(memory_space=pltpu.SMEM)
PARAMS = pltpu.CompilerParams(vmem_limit_bytes=24 * 1024 * 1024)

Q_HI, Q_LO, ROW, COL, NEXT_ROW, NEXT_COL = 0, 1, 2, 3, 4, 5
MEAN = (0, 1, 2)
W_CORE, W_ODD, ACTIVE, VALUE, ERROR, PLAN_ROW, PLAN_COL, PLAN_ROWS = 0, 3, 6, 7, 8, 9, 10, 16
NEAR, FAR, EVEN_Z, ODD_Z, EVEN_LAT = 0, 1, 2, 3, 4
EARLY = (NEAR, EVEN_Z)
LATE = (ODD_Z, FAR)


def call(kernel, name, out_shapes, operands, n_smem=0, scratch=()):
    return pl.pallas_call(
        kernel,
        name=name,
        out_shape=out_shapes,
        in_specs=[SMEM] * n_smem + [VMEM] * (len(operands) - n_smem),
        out_specs=jax.tree.map(lambda _: VMEM, out_shapes),
        scratch_shapes=list(scratch),
        compiler_params=PARAMS,
    )(*operands)


def shaped(shape, dtype=F32):
    return jax.ShapeDtypeStruct(shape, dtype)


def pick(cells, index):
    return jnp.take_along_axis(cells, index, axis=1, mode="promise_in_bounds")


def mean_of(cells):
    return jnp.sum(cells, axis=0, keepdims=True) * (1.0 / MEMB)


def lines(pairs, height):
    which = lax.broadcasted_iota(jnp.int32, (height, OBS), 0)
    table = jnp.zeros((height, OBS), F32)
    for k, line in pairs:
        table = jnp.where(which == k, line, table)
    return table


def halo_of(dev, mean):
    high = mean.astype(BF16).astype(F32)
    middle = (mean - high).astype(BF16).astype(F32)
    return dev, lines(zip(MEAN, (high, middle, mean - high - middle)), HEAD).astype(BF16)


def write_halos(even, first, last, core_ref, odd_ref):
    kept = []
    for cells in (first, last):
        mean = mean_of(cells)
        kept.append(((cells - mean).astype(BF16), mean))
    (dev_first, mean_first), (dev_last, mean_last) = kept
    for out_ref, swap in ((core_ref, True), (odd_ref, False)):
        a, b = (kept[1], kept[0]) if swap else (kept[0], kept[1])
        dev, head = halo_of(
            jnp.where(even, a[0].astype(F32), b[0].astype(F32)).astype(BF16), jnp.where(even, a[1], b[1])
        )
        out_ref[:MEMB] = dev
        out_ref[MEMB:] = head
    return dev_first, dev_last


def ends_kernel(first_ref, last_ref, core_ref, odd_ref):
    write_halos(lax.rem(lax.axis_index("lat"), 2) == 0, first_ref[...], last_ref[...], core_ref, odd_ref)


def write_plan(n_lat, order_ref, count_ref, value_ref, error_ref, row_ref, col_ref, foot_ref, plan_ref, inner_ref, place_ref):
    lat = lax.axis_index("lat")
    lon = lax.axis_index("lon")
    even = lax.rem(lat, 2) == 0
    not_first = (lat > 0).astype(F32)
    not_last = (lat < n_lat - 1).astype(F32)
    cell = lax.broadcasted_iota(jnp.int32, (1, CLON), 1)
    near = 1 - 2 * lax.rem(lon, 2)
    even_z = 2 - 4 * lax.rem(lax.div(lon, 2), 2)
    seen = [(cell - hop * CLON).astype(F32) for hop in (near, -near, even_z, -even_z)]
    parity = jnp.zeros((1, CLON), F32) + jnp.where(even, 1.0, 0.0)
    place_ref[...] = lines(zip((NEAR, FAR, EVEN_Z, ODD_Z, EVEN_LAT), (*seen, parity)), 8)
    cell_row = lax.broadcasted_iota(jnp.int32, (CLAT, OBS), 0)
    for step in range(NB):
        batch = order_ref[step]
        row = row_ref[batch]
        col = col_ref[batch]
        foot = [foot_ref[batch * 9 + k] for k in range(9)]
        inverse = 1.0 / sum(foot[1:], foot[0])
        foot = [weight * inverse for weight in foot]
        north = jnp.where(row == 0, not_first, 0.0)
        south = jnp.where(row == CLAT - 1, not_last, 0.0)
        entries = [
            (ACTIVE, (cell < count_ref[batch]).astype(F32)),
            (VALUE, value_ref[batch]),
            (ERROR, error_ref[batch]),
            (PLAN_ROW, row.astype(F32)),
            (PLAN_COL, col.astype(F32)),
        ]
        for dc in range(3):
            w_north = foot[dc] * north
            w_south = foot[6 + dc] * south
            entries.append((W_CORE + dc, jnp.where(even, w_south, w_north)))
            entries.append((W_ODD + dc, jnp.where(even, w_north, w_south)))
            weight = jnp.zeros((CLAT, OBS), F32)
            for dr in range(3):
                weight = weight + jnp.where(cell_row == row + (dr - 1), foot[3 * dr + dc], 0.0)
            inner_ref[step, dc] = weight
        plan_ref[step] = lines(entries, PLAN_ROWS)


def columns(plan, dc):
    col = plan[PLAN_COL : PLAN_COL + 1].astype(jnp.int32)
    return jnp.broadcast_to(col + (dc - 1), (MEMB, OBS))


def interior_prior(plan, inner_ref, step, read_row):
    total = jnp.zeros((MEMB, OBS), F32)
    for dc in range(3):
        index = columns(plan, dc)
        weight = inner_ref[step, dc]
        for r in range(CLAT):
            total = total + pick(read_row(r), index) * weight[r : r + 1]
    return total


def first_kernel(n_lat, *refs):
    given = refs[:8]
    state_ref, dev_ref, prior_ref, plan_ref, inner_ref, place_ref = refs[8:14]
    held = refs[14:22]
    sems = refs[22]
    half = CLAT // 2
    fetches = []
    for k in range(7):
        fetches.append(pltpu.make_async_copy(given[k], held[k], sems.at[k]))
    parts = []
    for k in range(2):
        rows = pl.ds(k * half, half)
        parts.append(pltpu.make_async_copy(given[7].at[:, rows], held[7].at[k], sems.at[7 + k]))
    for fetch in fetches + parts:
        fetch.start()
    for fetch in fetches:
        fetch.wait()
    write_plan(n_lat, *held[:7], plan_ref, inner_ref, place_ref)
    for k in range(2):
        parts[k].wait()
        for r in range(half):
            cells = held[7][k, :, r, :]
            state_ref[k * half + r] = cells
            dev_ref[k * half + r] = (cells - mean_of(cells)).astype(BF16)
    prior_ref[...] = interior_prior(plan_ref[0], inner_ref, 0, lambda r: state_ref[r])


def packet_kernel(step, plan_ref, prior_ref, core_ref, odd_ref, packet_ref):
    plan = plan_ref[step]
    later = plan_ref[min(step + 1, NB - 1)]
    total = prior_ref[...]
    for halo_ref, base in ((core_ref, W_CORE), (odd_ref, W_ODD)):
        head = halo_ref[MEMB:].astype(F32)
        mean = head[MEAN[0] : MEAN[0] + 1] + head[MEAN[1] : MEAN[1] + 1] + head[MEAN[2] : MEAN[2] + 1]
        cells = halo_ref[:MEMB].astype(F32) + mean
        for dc in range(3):
            total = total + pick(cells, columns(plan, dc)) * plan[base + dc : base + dc + 1]
    ybar = mean_of(total)
    dev = total - ybar
    spread = jnp.sum(dev * dev, axis=0, keepdims=True) * (1.0 / (MEMB - 1.0))
    error = plan[ERROR : ERROR + 1]
    inverse = 1.0 / (spread + error)
    widened = 1.0 + jnp.sqrt(error * inverse)
    scale = jnp.sqrt(plan[ACTIVE : ACTIVE + 1] * inverse / widened * (1.0 / (MEMB - 1.0)))
    pull = (plan[VALUE : VALUE + 1] - ybar) * (widened * scale)
    high = pull.astype(BF16).astype(F32)
    packet_ref[:MEMB] = (dev * scale).astype(BF16)
    packet_ref[MEMB:] = lines(
        (
            (Q_HI, high),
            (Q_LO, pull - high),
            (ROW, plan[PLAN_ROW : PLAN_ROW + 1]),
            (COL, plan[PLAN_COL : PLAN_COL + 1]),
            (NEXT_ROW, later[PLAN_ROW : PLAN_ROW + 1]),
            (NEXT_COL, later[PLAN_COL : PLAN_COL + 1]),
        ),
        HEAD,
    ).astype(BF16)


def tapers(packet_ref, cell, row_at, col_at):
    head = packet_ref[MEMB:].astype(F32).T
    row = head[:, row_at : row_at + 1]
    gap = (head[:, col_at : col_at + 1] - cell) * (1.0 / RADIUS)
    taper = jnp.maximum(0.0, 1.0 - gap * gap)
    size = 1.0 * CLAT * CLAT
    return taper * (1.0 - row * row / size), taper * (row * (2.0 / size)), taper * (1.0 / size)


def in_row(terms, r):
    a, b, c = terms
    return a if r == 0 else a + (1.0 * r) * (b - (1.0 * r) * c)


def step_of_rows(turned, packets, read_dev, read_taper, rows):
    dev = jnp.concatenate([read_dev(r) for r in rows], axis=1)
    covar = jnp.dot(turned, dev, preferred_element_type=F32)
    packed = []
    for k, r in enumerate(rows):
        packed.append((covar[:, k * CLON : (k + 1) * CLON] * read_taper(r)).astype(BF16))
    moved = jnp.dot(packets, jnp.concatenate(packed, axis=1), preferred_element_type=F32)
    step = moved[MEMB + Q_HI : MEMB + Q_HI + 1] + moved[MEMB + Q_LO : MEMB + Q_LO + 1] - moved[:MEMB]
    return [step[:, k * CLON : (k + 1) * CLON] for k in range(len(rows))]


def join(packet_refs):
    turned = jnp.concatenate([ref[:MEMB].T for ref in packet_refs], axis=0)
    packets = jnp.concatenate([ref[...] for ref in packet_refs], axis=1)
    return turned, packets


def inline_kernel(partners, place_ref, *refs):
    count = len(partners)
    packet_refs = refs[:count]
    dev_ref, state_ref, out_ref, terms_ref = refs[count:]
    for n, partner in enumerate(partners):
        if partner is None:
            cell = lax.broadcasted_iota(jnp.int32, (1, CLON), 1).astype(F32)
        else:
            cell = place_ref[partner : partner + 1]
        span = pl.ds(n * OBS, OBS)
        terms_ref[0, span], terms_ref[1, span], terms_ref[2, span] = tapers(packet_refs[n], cell, ROW, COL)
    turned, packets = join(packet_refs)
    for r in range(0, CLAT, 2):
        rows = (r, r + 1)
        steps = step_of_rows(
            turned, packets, lambda k: dev_ref[k], lambda k: in_row((terms_ref[0], terms_ref[1], terms_ref[2]), k), rows
        )
        for k, step in zip(rows, steps):
            out_ref[k] = state_ref[k] + step


def write_tapers(place_ref, packet_refs, row_at, col_at, taper_ref):
    for n, partner in enumerate(LATE):
        span = pl.ds(n * OBS, OBS)
        terms = tapers(packet_refs[n], place_ref[partner : partner + 1], row_at, col_at)
        for r in range(CLAT):
            taper_ref[r, span] = in_row(terms, r)


def taper_kernel(place_ref, a_ref, b_ref, state_ref, taper_ref):
    write_tapers(place_ref, (a_ref, b_ref), ROW, COL, taper_ref)


def edge_kernel(
    place_ref, a_ref, b_ref, taper_ref, dev_ref, state_ref, core_ref, odd_ref, edge_ref, edge_dev_ref, turned_ref
):
    turned, packets = join((a_ref, b_ref))
    turned_ref[...] = turned
    steps = step_of_rows(turned, packets, lambda k: dev_ref[k], lambda k: taper_ref[k], (0, CLAT - 1))
    first = state_ref[0] + steps[0]
    last = state_ref[CLAT - 1] + steps[1]
    edge_ref[0] = first
    edge_ref[1] = last
    even = place_ref[EVEN_LAT : EVEN_LAT + 1] > 0.5
    edge_dev_ref[0], edge_dev_ref[1] = write_halos(even, first, last, core_ref, odd_ref)


def rest_kernel(
    step, place_ref, plan_ref, inner_ref, a_ref, b_ref, turned_ref, taper_ref, dev_ref, state_ref, edge_ref, edge_dev_ref,
    out_ref, dev_out_ref, prior_ref, taper_out_ref,
):
    for k, r in ((0, 0), (1, CLAT - 1)):
        out_ref[r] = edge_ref[k]
        dev_out_ref[r] = edge_dev_ref[k]
    turned = turned_ref[...]
    packets = jnp.concatenate([a_ref[...], b_ref[...]], axis=1)
    for r in range(1, CLAT - 1, 2):
        rows = (r, r + 1)
        steps = step_of_rows(turned, packets, lambda k: dev_ref[k], lambda k: taper_ref[k], rows)
        for k, move in zip(rows, steps):
            cells = state_ref[k] + move
            out_ref[k] = cells
            dev_out_ref[k] = (cells - mean_of(cells)).astype(BF16)
    prior_ref[...] = interior_prior(plan_ref[step], inner_ref, step, lambda r: out_ref[r])
    write_tapers(place_ref, (a_ref, b_ref), NEXT_ROW, NEXT_COL, taper_out_ref)


def last_kernel(a_ref, b_ref, taper_ref, dev_ref, state_ref, out_ref):
    turned, packets = join((a_ref, b_ref))
    for r in range(0, CLAT, 2):
        rows = (r, r + 1)
        steps = step_of_rows(turned, packets, lambda k: dev_ref[k], lambda k: taper_ref[k], rows)
        for k, move in zip(rows, steps):
            out_ref[pl.ds(k, MEMB, stride=CLAT), :] = state_ref[k] + move


def local(ensemble, obs_value, obs_error, obs_row, obs_col, foot_weight, obs_count, batch_order):
    n_lon = lax.axis_size("lon")
    n_lat = lax.axis_size("lat")
    core_pairs = [(i, i ^ 1) for i in range(n_lat)]
    odd_pairs = [(i, (((i + 1) ^ 1) - 1) % n_lat) for i in range(n_lat)]
    pairs = {
        NEAR: [(i ^ 1, i) for i in range(n_lon)],
        FAR: [((((i + 1) ^ 1) - 1) % n_lon, i) for i in range(n_lon)],
        EVEN_Z: [(i ^ 2, i) for i in range(n_lon)],
        ODD_Z: [((((i + 2) ^ 2) - 2) % n_lon, i) for i in range(n_lon)],
    }

    def swap_lat(cells, pairs):
        return lax.ppermute(cells, "lat", pairs)

    cells = shaped((CLAT, MEMB, CLON))
    cells16 = shaped((CLAT, MEMB, CLON), BF16)
    plane = shaped((MEMB, CLON))
    halo = shaped((WIDE, CLON), BF16)
    taper_shape = shaped((CLAT, len(LATE) * OBS, CLON))

    core_end, odd_end = call(ends_kernel, "ends", (halo, halo), (ensemble[:, 0, :], ensemble[:, CLAT - 1, :]))
    odd_halo = swap_lat(odd_end, odd_pairs)
    core_halo = swap_lat(core_end, core_pairs)
    given = (
        batch_order, obs_count.reshape(NB), obs_value, obs_error, obs_row, obs_col,
        foot_weight.transpose(0, 2, 1, 3).reshape(NB * 9, 1, OBS), ensemble,
    )
    held = [pltpu.SMEM((NB,), jnp.int32)] * 2 + [pltpu.VMEM(given[k].shape, given[k].dtype) for k in range(2, 7)]
    held.append(pltpu.VMEM((2, MEMB, CLAT // 2, CLON), F32))
    state, dev, prior, plan, inner, place = pl.pallas_call(
        functools.partial(first_kernel, n_lat),
        name="first",
        out_shape=(
            cells, cells16, plane, shaped((NB, PLAN_ROWS, OBS)), shaped((NB, 3, CLAT, OBS)), shaped((8, CLON)),
        ),
        in_specs=[pl.BlockSpec(memory_space=pltpu.HBM)] * 8,
        out_specs=(VMEM,) * 6,
        scratch_shapes=[*held, pltpu.SemaphoreType.DMA((9,))],
        compiler_params=PARAMS,
    )(*[pltpu.with_memory_space_constraint(array, pltpu.HBM) for array in given])

    def moved(name, partners, packets, dev, state):
        scratch = [pltpu.VMEM((3, len(partners) * OBS, CLON), F32)]
        return call(
            functools.partial(inline_kernel, partners), name, cells, (place, *packets, dev, state), 0, scratch
        )

    taper = None
    for step in range(NB):
        packet = call(
            functools.partial(packet_kernel, step), "packet", halo, (plan, prior, core_halo, odd_halo)
        )
        arrived = {k: lax.ppermute(packet, "lon", pairs[k]) for k in (NEAR, EVEN_Z, ODD_Z, FAR)}
        late = [arrived[k] for k in LATE]
        state = moved("own", (None,), (packet,), dev, state)
        state = moved("early", EARLY, [arrived[k] for k in EARLY], dev, state)
        if step == 0:
            taper = call(taper_kernel, "taper", taper_shape, (place, *late, state))
        if step == NB - 1:
            flat = call(last_kernel, "last", shaped((MEMB * CLAT, CLON)), (*late, taper, dev, state))
            return flat.reshape(MEMB, CLAT, CLON)
        core_end, odd_end, edge, edge_dev, turned = call(
            edge_kernel,
            "edge",
            (
                halo,
                halo,
                shaped((2, MEMB, CLON)),
                shaped((2, MEMB, CLON), BF16),
                shaped((len(LATE) * OBS, MEMB), BF16),
            ),
            (place, *late, taper, dev, state),
        )
        odd_halo = swap_lat(odd_end, odd_pairs)
        core_halo = swap_lat(core_end, core_pairs)
        state, dev, prior, taper = call(
            functools.partial(rest_kernel, step + 1),
            "rest",
            (cells, cells16, plane, taper_shape),
            (place, plan, inner, *late, turned, taper, dev, state, edge, edge_dev),
        )


def solution(mesh):
    in_specs = (
        P(None, "lat", "lon"),
        P(None, "lat", "lon"),
        P(None, "lat", "lon"),
        P(None, "lat", "lon"),
        P(None, "lat", "lon"),
        P(None, "lat", None, "lon"),
        P(None, "lat", "lon"),
        P(),
    )
    out_specs = P(None, "lat", "lon")
    return jax.shard_map(local, mesh=mesh, in_specs=in_specs, out_specs=out_specs, check_vma=False)
```
